32 devices in a mesh: grp: 2 (over y), mem: 4 (over z), tile: 4 (over x, core).
Axes of the slice: x: 2, y: 2, z: 4, core: 2. Of those that a mesh axis runs over, the one named last changes fastest.
Arguments:
- state: bfloat16 [16, 1024, 256], P(('grp', 'mem'), 'tile'), parts along dimension 0, may hold values from -6 to 6
- op_blocks: bfloat16 [16, 128, 256], replicated, may hold values from -0.1875 to 0.1875
- block_kind: int32 [1024, 4], P(('grp', 'tile')), parts along dimension 0, may hold values from 0 to 15, all different within a row
- block_column: int32 [1024, 4], P(('grp', 'tile')), parts along dimension 0, may hold values from 0 to 255
- obs_value: float32 [8, 16384], P(('grp', 'tile'), 'mem'), parts along dimension 0, may hold values from -8 to 8
- obs_error: float32 [8, 16384], P(('grp', 'tile'), 'mem'), parts along dimension 0, may hold values from 0.5 to 2
- obs_frac: float32 [8, 16384], P(('grp', 'tile'), 'mem'), parts along dimension 0, may hold values from 0 to 1
- obs_count: int32 [8], P(('grp', 'tile')), parts along dimension 0, may hold values from 4096 to 16384, as said below
Outputs:
- gram: float32 [16, 4, 8], P(('grp', 'mem'), 'tile'), parts along dimension 0
- proj: float32 [16, 4], P(('grp', 'mem'), 'tile'), parts along dimension 0
The draws below stay inside these ranges and needn't reach their ends.
There are 2 independent parts, one for each index of `grp`. The reference program is written for one: setup_inputs(seed, part) draws one part's arguments, and reference() takes and returns one part's arrays. A program takes and returns all parts, laid end to end along the dimension named above; an argument that names none is the same for every part. Nothing has to cross between parts.
Inputs may be any that keep to these rules, and one draw needn't show every extreme that they name: `block_kind`: the 4 library entries of one observation block are distinct. `obs_count`: in every draw some tile has all 16384 observations live.
All inputs are finite; a program needn't handle non-finite values.
Results may differ from the reference program's by a relative error of at most 0.0033.
Values may be sent and summed in bfloat16 or wider, within the bound.
A program may use at most 64 MiB of HBM per device.

```python
import math
import jax
import jax.numpy as jnp
from jax import lax

VB = 256
OB = 128
K = 4
NKIND = 16
VBLK = 256
MEMBERS = 8
TILES = 4
OBT = 128


def draw_obs_count(key, part):
    key = jax.random.fold_in(key, 7)
    first_key, second_key = jax.random.split(key)
    full_rows = OBT * OB
    counts = jax.random.randint(first_key, (TILES,), full_rows // 4, full_rows + 1)
    chosen = jax.random.randint(second_key, (), 0, TILES)
    return jnp.where(jnp.arange(TILES) == chosen, full_rows, counts).astype(jnp.int32)


def touch_ends(array, rng, smallest, high):
    extent = array.shape
    spot = [jax.random.randint(jax.random.fold_in(rng, axis), (), 0, extent[axis]) for axis in range(len(extent))]
    array = array.at[tuple(spot)].set(smallest)
    longest = extent.index(max(extent))
    spot[longest] = (spot[longest] + 1) % extent[longest]
    return array.at[tuple(spot)].set(high)


def levels(own_key, shape, shards, smallest, high):
    loudness, own = 1.0, jax.random.fold_in(own_key, 6)
    for dim, parts in shards:
        steps = jnp.exp(jax.random.uniform(jax.random.fold_in(own, dim), (parts,), jnp.float32, smallest / len(shards), high / len(shards)))
        loudness = loudness * jnp.repeat(steps, shape[dim] // parts).reshape([-1 if axis == dim else 1 for axis in range(len(shape))])
    return loudness


def picks_of(key, rows, number_of, top, lift):
    order = jax.random.permutation(jax.random.fold_in(key, 1), number_of)
    pull = order
    for power in range(3):
        pull = pull * pull // number_of
    pull = pull * lift // number_of
    chance = jax.random.randint(jax.random.fold_in(key, 2), (rows, number_of), 0, 4096) + pull
    fixed_rows = jax.random.permutation(jax.random.fold_in(key, 3), rows)[jnp.arange(number_of) % rows]
    chance = jnp.where(jnp.arange(rows)[:, None] == fixed_rows[None, :], 1 << 14, chance)
    merit = chance * number_of + jnp.arange(number_of)
    return lax.top_k(merit.astype(jnp.int32), top)[1].astype(jnp.int32)


def scatter_about(key, extent, deviation, reach, shards=(), kind=jnp.bfloat16):
    loudness = levels(key, extent, shards, -0.22, 0.18) if shards else 1.0
    result = jax.random.normal(key, extent, jnp.float32) * deviation * loudness
    return jnp.minimum(jnp.maximum(result, -reach), reach).astype(kind)


def setup_inputs(seed: int = 0, part: int = 0) -> dict:
    splits = jax.random.split(jax.random.key(seed), 9)
    part_splits = jax.random.split(jax.random.fold_in(splits[8], part), 9)
    state = scatter_about(part_splits[0], (MEMBERS, TILES * VBLK, VB), 1.0, 6.0, ((0, 4), (1, 4)))
    op_blocks = scatter_about(splits[1], (NKIND, OB, VB), (K * VB) ** -0.5, 0.1875)
    block_kind = picks_of(part_splits[2], (TILES * OBT), NKIND, K, 0)
    block_column = touch_ends(jax.random.randint(part_splits[3], (TILES * OBT, K), 0, VBLK), jax.random.fold_in(part_splits[3], 1), 0, VBLK - 1).astype(jnp.int32)
    obs_value = scatter_about(part_splits[4], (TILES, OBT * OB), 1.5, 8.0, ((0, 4), (1, 4)), jnp.float32)
    obs_error = jnp.clip(jnp.exp(math.log(2.0) - 1.3862944 * jax.random.uniform(part_splits[5], (TILES, OBT * OB), jnp.float32) ** levels(part_splits[5], (TILES, OBT * OB), ((0, 4), (1, 4)), -0.2, 0.2)), 0.5, 2.0)
    obs_frac = jnp.clip(1.0 * jax.random.uniform(part_splits[6], (TILES, OBT * OB), jnp.float32) ** levels(part_splits[6], (TILES, OBT * OB), ((0, 4), (1, 4)), -0.2, 0.2), 0.0, 1.0)
    obs_count = draw_obs_count(jax.random.fold_in(jax.random.fold_in(splits[8], part), 71), part)
    return {"state": state, "op_blocks": op_blocks, "block_kind": block_kind, "block_column": block_column, "obs_value": obs_value, "obs_error": obs_error, "obs_frac": obs_frac, "obs_count": obs_count}


def reference(state, op_blocks, block_kind, block_column, obs_value, obs_error, obs_frac, obs_count):
    lookup_table = jnp.transpose(op_blocks, (2, 0, 1)).reshape(VB, NKIND * OB)
    tile_state = jnp.transpose(state.reshape(MEMBERS, TILES, VBLK, VB), (1, 0, 2, 3))
    kinds = block_kind.reshape(TILES, OBT, K)
    columns = block_column.reshape(TILES, OBT, K)

    def tile_priors(inputs):
        member_states, tile_kinds, tile_columns = inputs
        flat_index = (tile_columns * NKIND + tile_kinds).reshape(-1).astype(jnp.int32)

        def member_priors(member_state):
            product = jnp.dot(member_state, lookup_table, preferred_element_type=jnp.float32)
            product = product.reshape(VBLK * NKIND, OB)
            picked = jnp.take(product, flat_index, axis=0).reshape(OBT, K, OB)
            return jnp.sum(picked, axis=1).reshape(OBT * OB).astype(jnp.bfloat16)

        return lax.map(member_priors, member_states)

    prior_obs = lax.map(tile_priors, (tile_state, kinds, columns))
    member_mean = jnp.mean(prior_obs.astype(jnp.float32), axis=1)
    perturbed = (prior_obs.astype(jnp.float32) - member_mean[:, None, :]).astype(jnp.bfloat16)
    innovation = obs_value - member_mean
    row_index = jnp.arange(OBT * OB, dtype=jnp.int32)
    live_mask = row_index[None, :] < obs_count[:, None]
    inv_var = jnp.where(live_mask, 1.0 / (obs_error * obs_error), 0.0)
    position = jnp.arange(TILES, dtype=jnp.float32)[:, None] + obs_frac
    radius = TILES / 4.0
    obs_total = float(TILES * OBT * OB)
    groups = OBT * OB // 1024
    pert_blocks = jnp.transpose(perturbed.reshape(TILES, MEMBERS, groups, 1024), (0, 2, 1, 3)).reshape(TILES * groups, MEMBERS, 1024)
    pos_blocks = position.reshape(TILES * groups, 1024)
    inv_blocks = inv_var.reshape(TILES * groups, 1024)
    inn_blocks = innovation.reshape(TILES * groups, 1024)
    targets = jnp.arange(TILES, dtype=jnp.float32) + 0.5

    def block_step(running, inputs):
        gram_acc, proj_acc = running
        block_pert, block_pos, block_inv, block_innovation = inputs
        spread = jnp.abs(block_pos[None, :] - targets[:, None])
        distance = jnp.minimum(spread, TILES - spread)
        inflation_factor = block_inv[None, :] / (1.0 + (distance / radius) ** 2) / obs_total
        pert_wide = block_pert.astype(jnp.float32)
        weighted = (pert_wide[None, :, :] * inflation_factor[:, None, :]).astype(jnp.bfloat16)
        gram_acc = gram_acc + jnp.einsum("tar,cr->atc", weighted.astype(jnp.float32), pert_wide, precision=lax.Precision.HIGHEST)
        proj_acc = proj_acc + jnp.einsum("ar,tr->at", pert_wide, inflation_factor * block_innovation[None, :], precision=lax.Precision.HIGHEST)
        return (gram_acc, proj_acc), None

    initial_state = (jnp.zeros((MEMBERS, TILES, MEMBERS), jnp.float32), jnp.zeros((MEMBERS, TILES), jnp.float32))
    (gram, proj), unused = lax.scan(block_step, initial_state, (pert_blocks, pos_blocks, inv_blocks, inn_blocks))
    return gram, proj
```

```python
import functools

import jax
import jax.numpy as jnp
from jax import lax
from jax.experimental import pallas as pl
from jax.experimental.pallas import tpu as pltpu
from jax.sharding import PartitionSpec as P

MESH = pl.DeviceIdType.MESH
UNROLL_LIMIT = 16
F32 = jnp.float32
BF16 = jnp.bfloat16


def each(start, stop, body):
    if stop - start <= UNROLL_LIMIT:
        for i in range(start, stop):
            body(i)
    else:

        def step(i, carry):
            body(i)
            return carry

        lax.fori_loop(start, stop, step, 0)


def kernel(
    n_mem, n_tile, lib_chunks, block_chunk,
    count_ref, state_hbm, lib_hbm, kind_hbm, column_hbm, value_hbm, error_hbm, frac_hbm,
    gram_ref, proj_ref,
    state_ref, lib_ref, kind_ref, column_ref, value_ref, error_ref, frac_ref,
    prior_ref, regrouped_ref, factor_ref, mean_ref, pert_ref, pert16_ref, weighted_ref,
    piece_ref, landed_ref,
    load_sem, lib_sem, send_sem, recv_sem, piece_send_sem, piece_recv_sem,
):
    mem_dev, value_rows, _ = state_ref.shape
    kind_count, obs_width, _ = lib_ref.shape
    per_block, tile_blocks = kind_ref.shape
    own_blocks = tile_blocks // n_mem
    row_count = own_blocks * obs_width
    members = n_mem * mem_dev
    group = n_mem * n_tile
    mem_id = lax.axis_index("mem")
    tile_id = lax.axis_index("tile")
    me = mem_id * n_tile + tile_id

    loads = [
        pltpu.make_async_copy(src, dst, load_sem.at[i])
        for i, (src, dst) in enumerate(
            (
                (kind_hbm, kind_ref), (column_hbm, column_ref), (state_hbm, state_ref),
                (value_hbm, value_ref), (error_hbm, error_ref), (frac_hbm, frac_ref),
            )
        )
    ]
    per_chunk = kind_count // lib_chunks
    lib_loads = [
        pltpu.make_async_copy(
            lib_hbm.at[pl.ds(i * per_chunk, per_chunk)],
            lib_ref.at[pl.ds(i * per_chunk, per_chunk)],
            lib_sem.at[i],
        )
        for i in range(lib_chunks)
    ]
    for copy in loads[:3] + lib_loads + loads[3:]:
        copy.start()

    barrier = pltpu.get_barrier_semaphore()

    def coordinates(shift):
        peer = lax.rem(me + shift, group)
        return peer, peer // n_tile, lax.rem(peer, n_tile)

    def greet(shift):
        _, peer_mem, peer_tile = coordinates(shift)
        pl.semaphore_signal(
            barrier, inc=1, device_id={"mem": peer_mem, "tile": peer_tile}, device_id_type=MESH
        )

    each(1, group, greet)

    loads[0].wait()
    loads[1].wait()
    loads[2].wait()

    def priors(first_block, wait_lib):
        kinds = kind_ref[:, pl.ds(first_block, block_chunk)]
        columns = column_ref[:, pl.ds(first_block, block_chunk)]
        entry = lax.broadcasted_iota(jnp.int32, (kind_count, block_chunk), 0)
        chosen = jnp.full((kind_count, block_chunk), -1, jnp.int32)
        for k in range(per_block):
            chosen = jnp.where(kinds[k : k + 1, :] == entry, columns[k : k + 1, :], chosen)
        chosen = jnp.transpose(chosen.astype(F32), (1, 0))
        lane = lax.broadcasted_iota(jnp.int32, (block_chunk, value_rows), 1).astype(F32)
        total = jnp.zeros((mem_dev * block_chunk, obs_width), F32)
        for j in range(kind_count):
            pick = jnp.where(chosen[:, j : j + 1] == lane, 1.0, 0.0).astype(BF16)
            picked = jnp.concatenate(
                [
                    jnp.dot(pick, state_ref[m], preferred_element_type=F32).astype(BF16)
                    for m in range(mem_dev)
                ],
                axis=0,
            )
            if wait_lib and j % per_chunk == 0:
                lib_loads[j // per_chunk].wait()
            total = total + lax.dot_general(
                picked, lib_ref[j], (((1,), (1,)), ((), ())), preferred_element_type=F32
            )
        total = total.astype(BF16).reshape(mem_dev, block_chunk, obs_width)
        prior_ref[:, pl.ds(first_block, block_chunk), :] = total

    if tile_blocks == block_chunk:
        priors(0, True)
    else:
        for copy in lib_loads:
            copy.wait()
        each(0, tile_blocks // block_chunk, lambda i: priors(i * block_chunk, False))

    pl.semaphore_wait(barrier, group - 1)

    def regroup(shift):
        peer = lax.rem(mem_id + shift, n_mem)
        return pltpu.make_async_remote_copy(
            src_ref=prior_ref.at[:, pl.ds(pl.multiple_of(peer * own_blocks, own_blocks), own_blocks), :],
            dst_ref=regrouped_ref.at[mem_id],
            send_sem=send_sem.at[peer],
            recv_sem=recv_sem.at[mem_id],
            device_id={"mem": peer},
            device_id_type=MESH,
        )

    def arriving(shift):
        peer = lax.rem(mem_id + shift, n_mem)
        return pltpu.make_async_remote_copy(
            src_ref=prior_ref.at[:, pl.ds(pl.multiple_of(peer * own_blocks, own_blocks), own_blocks), :],
            dst_ref=regrouped_ref.at[peer],
            send_sem=send_sem.at[peer],
            recv_sem=recv_sem.at[peer],
            device_id={"mem": peer},
            device_id_type=MESH,
        )

    each(1, n_mem, lambda shift: regroup(shift).start())
    regrouped_ref[mem_id] = prior_ref[:, pl.ds(pl.multiple_of(mem_id * own_blocks, own_blocks), own_blocks), :]

    for copy in loads[3:]:
        copy.wait()
    target = lax.broadcasted_iota(jnp.int32, (n_tile, row_count), 0).astype(F32) + 0.5
    position = tile_id.astype(F32) + frac_ref[...]
    spread = jnp.abs(position - target)
    distance = jnp.minimum(spread, n_tile - spread) / (n_tile / 4.0)
    error = error_ref[...]
    live = mem_id * row_count + lax.broadcasted_iota(jnp.int32, (1, row_count), 1) < count_ref[0]
    inv_var = jnp.where(live, 1.0 / (error * error), 0.0)
    obs_total = float(n_tile * tile_blocks * obs_width)
    factor_ref[...] = inv_var / (1.0 + distance * distance) / obs_total

    each(1, n_mem, lambda shift: arriving(shift).wait_recv())

    observed = regrouped_ref[...].astype(F32).reshape(members, own_blocks, obs_width)
    mean = jnp.sum(observed, axis=0) / members
    mean_ref[...] = mean
    pert = (observed - mean[None]).astype(BF16).astype(F32)
    pert_ref[...] = pert.reshape(members * own_blocks, obs_width)

    proj = [jnp.zeros((members, obs_width), F32) for _ in range(n_tile)]
    for b in range(own_blocks):
        lanes = slice(b * obs_width, (b + 1) * obs_width)
        block = pert_ref[pl.ds(b, members, stride=own_blocks), :]
        factor = factor_ref[:, lanes]
        innovation = value_ref[:, lanes] - mean_ref[b : b + 1, :]
        pull = factor * innovation
        pert16_ref[:, lanes] = block.astype(BF16)
        weighted_ref[:, lanes] = jnp.concatenate(
            [block * factor[s : s + 1, :] for s in range(n_tile)], axis=0
        ).astype(BF16)
        for s in range(n_tile):
            proj[s] = proj[s] + block * pull[s : s + 1, :]
    gram = lax.dot_general(
        weighted_ref[...], pert16_ref[...], (((1,), (1,)), ((), ())), preferred_element_type=F32
    )
    for s in range(n_tile):
        sums = jnp.sum(proj[s], axis=1, keepdims=True)
        for i in range(n_mem):
            rows = slice(i * mem_dev, (i + 1) * mem_dev)
            piece_ref[s, i, :, 0:members] = gram[s * members : (s + 1) * members][rows]
            piece_ref[s, i, :, members : members + 1] = sums[rows]

    def share(shift):
        peer, peer_mem, peer_tile = coordinates(shift)
        return pltpu.make_async_remote_copy(
            src_ref=piece_ref.at[peer_tile, peer_mem],
            dst_ref=landed_ref.at[me],
            send_sem=piece_send_sem.at[peer],
            recv_sem=piece_recv_sem.at[me],
            device_id={"mem": peer_mem, "tile": peer_tile},
            device_id_type=MESH,
        )

    def share_arriving(shift):
        peer, peer_mem, peer_tile = coordinates(shift)
        return pltpu.make_async_remote_copy(
            src_ref=piece_ref.at[peer_tile, peer_mem],
            dst_ref=landed_ref.at[peer],
            send_sem=piece_send_sem.at[peer],
            recv_sem=piece_recv_sem.at[peer],
            device_id={"mem": peer_mem, "tile": peer_tile},
            device_id_type=MESH,
        )

    each(1, group, lambda shift: share(shift).start())
    landed_ref[me] = piece_ref[tile_id, mem_id]
    each(1, n_mem, lambda shift: regroup(shift).wait_send())
    each(1, group, lambda shift: share_arriving(shift).wait_recv())
    result = jnp.sum(landed_ref[...], axis=0)
    gram_ref[...] = result[:, None, 0:members]
    for m in range(mem_dev):
        proj_ref[0:1, m : m + 1] = result[m : m + 1, members : members + 1]
    each(1, group, lambda shift: share(shift).wait_send())


def on_device(
    state, op_blocks, block_kind, block_column, obs_value, obs_error, obs_frac, obs_count
):
    n_mem = lax.axis_size("mem")
    n_tile = lax.axis_size("tile")
    mem_dev = state.shape[0]
    kind_count, obs_width, _ = op_blocks.shape
    tile_blocks, per_block = block_kind.shape
    own_blocks = tile_blocks // n_mem
    row_count = own_blocks * obs_width
    members = n_mem * mem_dev
    group = n_mem * n_tile
    lib_chunks = 4 if kind_count % 4 == 0 else 1
    block_chunk = 128 if tile_blocks % 128 == 0 else tile_blocks
    piece_width = -(-(members + 1) // 128) * 128
    anywhere = pl.BlockSpec(memory_space=pl.ANY)
    gram, proj = pl.pallas_call(
        functools.partial(kernel, n_mem, n_tile, lib_chunks, block_chunk),
        out_shape=(
            jax.ShapeDtypeStruct((mem_dev, 1, members), F32),
            jax.ShapeDtypeStruct((1, mem_dev), F32),
        ),
        in_specs=[pl.BlockSpec(memory_space=pltpu.SMEM)] + [anywhere] * 7,
        out_specs=(
            pl.BlockSpec(memory_space=pltpu.VMEM),
            pl.BlockSpec(memory_space=pltpu.VMEM),
        ),
        scratch_shapes=[
            pltpu.VMEM(state.shape, BF16),
            pltpu.VMEM(op_blocks.shape, BF16),
            pltpu.VMEM((per_block, tile_blocks), jnp.int32),
            pltpu.VMEM((per_block, tile_blocks), jnp.int32),
            pltpu.VMEM((1, row_count), F32),
            pltpu.VMEM((1, row_count), F32),
            pltpu.VMEM((1, row_count), F32),
            pltpu.VMEM((mem_dev, tile_blocks, obs_width), BF16),
            pltpu.VMEM((n_mem, mem_dev, own_blocks, obs_width), BF16),
            pltpu.VMEM((n_tile, row_count), F32),
            pltpu.VMEM((own_blocks, obs_width), F32),
            pltpu.VMEM((members * own_blocks, obs_width), F32),
            pltpu.VMEM((members, row_count), BF16),
            pltpu.VMEM((n_tile * members, row_count), BF16),
            pltpu.VMEM((n_tile, n_mem, mem_dev, piece_width), F32),
            pltpu.VMEM((group, mem_dev, piece_width), F32),
            pltpu.SemaphoreType.DMA((6,)),
            pltpu.SemaphoreType.DMA((lib_chunks,)),
            pltpu.SemaphoreType.DMA((n_mem,)),
            pltpu.SemaphoreType.DMA((n_mem,)),
            pltpu.SemaphoreType.DMA((group,)),
            pltpu.SemaphoreType.DMA((group,)),
        ],
        compiler_params=pltpu.CompilerParams(
            collective_id=0, has_side_effects=True, vmem_limit_bytes=40 * 1024 * 1024
        ),
    )(
        obs_count, state, op_blocks, jnp.transpose(block_kind), jnp.transpose(block_column),
        obs_value, obs_error, obs_frac,
    )
    return gram, jnp.transpose(proj)


def solution(mesh):
    return jax.shard_map(
        on_device,
        mesh=mesh,
        in_specs=(
            P(("grp", "mem"), "tile", None),
            P(),
            P(("grp", "tile"), None),
            P(("grp", "tile"), None),
            P(("grp", "tile"), "mem"),
            P(("grp", "tile"), "mem"),
            P(("grp", "tile"), "mem"),
            P(("grp", "tile")),
        ),
        out_specs=(P(("grp", "mem"), "tile", None), P(("grp", "mem"), "tile")),
        check_vma=False,
    )
```

```python
import functools

import jax
import jax.numpy as jnp
from jax import lax
from jax.experimental import pallas as pl
from jax.experimental.pallas import tpu as pltpu
from jax.sharding import PartitionSpec as P

MESH = pl.DeviceIdType.MESH
UNROLL_LIMIT = 16
F32 = jnp.float32
BF16 = jnp.bfloat16


def each(start, stop, body):
    if stop - start <= UNROLL_LIMIT:
        for i in range(start, stop):
            body(i)
    else:

        def step(i, carry):
            body(i)
            return carry

        lax.fori_loop(start, stop, step, 0)


def kernel(
    n_mem, n_tile, lib_chunks, block_chunk,
    count_hbm, state_hbm, lib_hbm, kind_hbm, column_hbm, value_hbm, error_hbm, frac_hbm,
    result_ref,
    count_ref, state_ref, lib_ref, kind_ref, column_ref, value_ref, error_ref, frac_ref,
    prior_ref, regrouped_ref, factor_ref, mean_ref, pert_ref, pert16_ref, weighted_ref,
    piece_ref, landed_ref,
    load_sem, lib_sem, send_sem, recv_sem, piece_send_sem, piece_recv_sem,
):
    mem_dev, value_rows, _ = state_ref.shape
    kind_count, obs_width, _ = lib_ref.shape
    per_block, tile_blocks = kind_ref.shape
    own_blocks = tile_blocks // n_mem
    row_count = own_blocks * obs_width
    members = n_mem * mem_dev
    group = n_mem * n_tile
    mem_id = lax.axis_index("mem")
    tile_id = lax.axis_index("tile")
    me = mem_id * n_tile + tile_id

    loads = [
        pltpu.make_async_copy(src, dst, load_sem.at[i])
        for i, (src, dst) in enumerate(
            (
                (kind_hbm, kind_ref), (column_hbm, column_ref), (state_hbm, state_ref),
                (value_hbm, value_ref), (error_hbm, error_ref), (frac_hbm, frac_ref),
                (count_hbm, count_ref),
            )
        )
    ]
    per_chunk = kind_count // lib_chunks
    lib_loads = [
        pltpu.make_async_copy(
            lib_hbm.at[pl.ds(i * per_chunk, per_chunk)],
            lib_ref.at[pl.ds(i * per_chunk, per_chunk)],
            lib_sem.at[i],
        )
        for i in range(lib_chunks)
    ]
    for copy in loads[:3] + lib_loads + loads[3:]:
        copy.start()

    barrier = pltpu.get_barrier_semaphore()

    def coordinates(shift):
        peer = lax.rem(me + shift, group)
        return peer, peer // n_tile, lax.rem(peer, n_tile)

    def greet(shift):
        _, peer_mem, peer_tile = coordinates(shift)
        pl.semaphore_signal(
            barrier, inc=1, device_id={"mem": peer_mem, "tile": peer_tile}, device_id_type=MESH
        )

    each(1, group, greet)

    loads[0].wait()
    loads[1].wait()
    loads[2].wait()

    def priors(first_block, wait_lib):
        kinds = kind_ref[:, pl.ds(first_block, block_chunk)]
        columns = column_ref[:, pl.ds(first_block, block_chunk)]
        entry = lax.broadcasted_iota(jnp.int32, (kind_count, block_chunk), 0)
        chosen = jnp.full((kind_count, block_chunk), -1, jnp.int32)
        for k in range(per_block):
            chosen = jnp.where(kinds[k : k + 1, :] == entry, columns[k : k + 1, :], chosen)
        chosen = jnp.transpose(chosen.astype(F32), (1, 0))
        lane = lax.broadcasted_iota(jnp.int32, (block_chunk, value_rows), 1).astype(F32)
        total = jnp.zeros((mem_dev * block_chunk, obs_width), F32)
        for j in range(kind_count):
            pick = jnp.where(chosen[:, j : j + 1] == lane, 1.0, 0.0).astype(BF16)
            picked = jnp.concatenate(
                [
                    jnp.dot(pick, state_ref[m], preferred_element_type=F32).astype(BF16)
                    for m in range(mem_dev)
                ],
                axis=0,
            )
            if wait_lib and j % per_chunk == 0:
                lib_loads[j // per_chunk].wait()
            total = total + lax.dot_general(
                picked, lib_ref[j], (((1,), (1,)), ((), ())), preferred_element_type=F32
            )
        total = total.astype(BF16).reshape(mem_dev, block_chunk, obs_width)
        prior_ref[:, pl.ds(first_block, block_chunk), :] = total

    if tile_blocks == block_chunk:
        priors(0, True)
    else:
        for copy in lib_loads:
            copy.wait()
        each(0, tile_blocks // block_chunk, lambda i: priors(i * block_chunk, False))

    pl.semaphore_wait(barrier, group - 1)

    def regroup(shift):
        peer = lax.rem(mem_id + shift, n_mem)
        return pltpu.make_async_remote_copy(
            src_ref=prior_ref.at[:, pl.ds(pl.multiple_of(peer * own_blocks, own_blocks), own_blocks), :],
            dst_ref=regrouped_ref.at[mem_id],
            send_sem=send_sem.at[peer],
            recv_sem=recv_sem.at[mem_id],
            device_id={"mem": peer},
            device_id_type=MESH,
        )

    def arriving(shift):
        peer = lax.rem(mem_id + shift, n_mem)
        return pltpu.make_async_remote_copy(
            src_ref=prior_ref.at[:, pl.ds(pl.multiple_of(peer * own_blocks, own_blocks), own_blocks), :],
            dst_ref=regrouped_ref.at[peer],
            send_sem=send_sem.at[peer],
            recv_sem=recv_sem.at[peer],
            device_id={"mem": peer},
            device_id_type=MESH,
        )

    each(1, n_mem, lambda shift: regroup(shift).start())
    regrouped_ref[mem_id] = prior_ref[:, pl.ds(pl.multiple_of(mem_id * own_blocks, own_blocks), own_blocks), :]

    for copy in loads[3:]:
        copy.wait()
    target = lax.broadcasted_iota(jnp.int32, (n_tile, row_count), 0).astype(F32) + 0.5
    position = tile_id.astype(F32) + frac_ref[...]
    spread = jnp.abs(position - target)
    distance = jnp.minimum(spread, n_tile - spread) / (n_tile / 4.0)
    error = error_ref[...]
    live = mem_id * row_count + lax.broadcasted_iota(jnp.int32, (1, row_count), 1) < count_ref[...]
    inv_var = jnp.where(live, 1.0 / (error * error), 0.0)
    obs_total = float(n_tile * tile_blocks * obs_width)
    factor_ref[...] = inv_var / (1.0 + distance * distance) / obs_total

    each(1, n_mem, lambda shift: arriving(shift).wait_recv())

    observed = regrouped_ref[...].astype(F32).reshape(members, own_blocks, obs_width)
    mean = jnp.sum(observed, axis=0) / members
    mean_ref[...] = mean
    pert = (observed - mean[None]).astype(BF16).astype(F32)
    pert_ref[...] = pert.reshape(members * own_blocks, obs_width)

    proj = [jnp.zeros((members, obs_width), F32) for _ in range(n_tile)]
    for b in range(own_blocks):
        lanes = slice(b * obs_width, (b + 1) * obs_width)
        block = pert_ref[pl.ds(b, members, stride=own_blocks), :]
        factor = factor_ref[:, lanes]
        innovation = value_ref[:, lanes] - mean_ref[b : b + 1, :]
        pull = factor * innovation
        pert16_ref[:, lanes] = block.astype(BF16)
        weighted_ref[:, lanes] = jnp.concatenate(
            [block * factor[s : s + 1, :] for s in range(n_tile)], axis=0
        ).astype(BF16)
        for s in range(n_tile):
            proj[s] = proj[s] + block * pull[s : s + 1, :]
    gram = lax.dot_general(
        weighted_ref[...], pert16_ref[...], (((1,), (1,)), ((), ())), preferred_element_type=F32
    )
    for s in range(n_tile):
        sums = jnp.sum(proj[s], axis=1, keepdims=True)
        for i in range(n_mem):
            rows = slice(i * mem_dev, (i + 1) * mem_dev)
            piece_ref[s, i, :, 0:members] = gram[s * members : (s + 1) * members][rows]
            piece_ref[s, i, :, members : members + 1] = sums[rows]

    def share(shift):
        peer, peer_mem, peer_tile = coordinates(shift)
        return pltpu.make_async_remote_copy(
            src_ref=piece_ref.at[peer_tile, peer_mem],
            dst_ref=landed_ref.at[me],
            send_sem=piece_send_sem.at[peer],
            recv_sem=piece_recv_sem.at[me],
            device_id={"mem": peer_mem, "tile": peer_tile},
            device_id_type=MESH,
        )

    def share_arriving(shift):
        peer, peer_mem, peer_tile = coordinates(shift)
        return pltpu.make_async_remote_copy(
            src_ref=piece_ref.at[peer_tile, peer_mem],
            dst_ref=landed_ref.at[peer],
            send_sem=piece_send_sem.at[peer],
            recv_sem=piece_recv_sem.at[peer],
            device_id={"mem": peer_mem, "tile": peer_tile},
            device_id_type=MESH,
        )

    each(1, group, lambda shift: share(shift).start())
    landed_ref[me] = piece_ref[tile_id, mem_id]
    each(1, n_mem, lambda shift: regroup(shift).wait_send())
    each(1, group, lambda shift: share_arriving(shift).wait_recv())
    result = jnp.sum(landed_ref[...], axis=0)
    result_ref[0:mem_dev, :] = result
    for m in range(mem_dev):
        result_ref[mem_dev : mem_dev + 1, m : m + 1] = result[m : m + 1, members : members + 1]
    each(1, group, lambda shift: share(shift).wait_send())


def on_device(
    state, op_blocks, block_kind, block_column, obs_value, obs_error, obs_frac, obs_count
):
    n_mem = lax.axis_size("mem")
    n_tile = lax.axis_size("tile")
    mem_dev = state.shape[0]
    kind_count, obs_width, _ = op_blocks.shape
    tile_blocks, per_block = block_kind.shape
    own_blocks = tile_blocks // n_mem
    row_count = own_blocks * obs_width
    members = n_mem * mem_dev
    group = n_mem * n_tile
    lib_chunks = 4 if kind_count % 4 == 0 else 1
    block_chunk = 128 if tile_blocks % 128 == 0 else tile_blocks
    piece_width = -(-(members + 1) // 128) * 128
    in_hbm = pl.BlockSpec(memory_space=pltpu.HBM)
    result = pl.pallas_call(
        functools.partial(kernel, n_mem, n_tile, lib_chunks, block_chunk),
        out_shape=jax.ShapeDtypeStruct((mem_dev + 1, piece_width), F32),
        in_specs=[in_hbm] * 8,
        out_specs=pl.BlockSpec(memory_space=pltpu.VMEM),
        scratch_shapes=[
            pltpu.VMEM((1, 1), jnp.int32),
            pltpu.VMEM(state.shape, BF16),
            pltpu.VMEM(op_blocks.shape, BF16),
            pltpu.VMEM((per_block, tile_blocks), jnp.int32),
            pltpu.VMEM((per_block, tile_blocks), jnp.int32),
            pltpu.VMEM((1, row_count), F32),
            pltpu.VMEM((1, row_count), F32),
            pltpu.VMEM((1, row_count), F32),
            pltpu.VMEM((mem_dev, tile_blocks, obs_width), BF16),
            pltpu.VMEM((n_mem, mem_dev, own_blocks, obs_width), BF16),
            pltpu.VMEM((n_tile, row_count), F32),
            pltpu.VMEM((own_blocks, obs_width), F32),
            pltpu.VMEM((members * own_blocks, obs_width), F32),
            pltpu.VMEM((members, row_count), BF16),
            pltpu.VMEM((n_tile * members, row_count), BF16),
            pltpu.VMEM((n_tile, n_mem, mem_dev, piece_width), F32),
            pltpu.VMEM((group, mem_dev, piece_width), F32),
            pltpu.SemaphoreType.DMA((7,)),
            pltpu.SemaphoreType.DMA((lib_chunks,)),
            pltpu.SemaphoreType.DMA((n_mem,)),
            pltpu.SemaphoreType.DMA((n_mem,)),
            pltpu.SemaphoreType.DMA((group,)),
            pltpu.SemaphoreType.DMA((group,)),
        ],
        compiler_params=pltpu.CompilerParams(
            collective_id=0, has_side_effects=True, vmem_limit_bytes=64 * 1024 * 1024
        ),
    )(
        obs_count.reshape(1, 1), state, op_blocks, jnp.transpose(block_kind), jnp.transpose(block_column),
        obs_value, obs_error, obs_frac,
    )
    return result[:mem_dev, None, :members], jnp.transpose(result[mem_dev:, :mem_dev])


def solution(mesh):
    return jax.shard_map(
        on_device,
        mesh=mesh,
        in_specs=(
            P(("grp", "mem"), "tile", None),
            P(),
            P(("grp", "tile"), None),
            P(("grp", "tile"), None),
            P(("grp", "tile"), "mem"),
            P(("grp", "tile"), "mem"),
            P(("grp", "tile"), "mem"),
            P(("grp", "tile")),
        ),
        out_specs=(P(("grp", "mem"), "tile", None), P(("grp", "mem"), "tile")),
        check_vma=False,
    )
```

```python
import functools

import jax
import jax.numpy as jnp
from jax import lax
from jax.experimental import pallas as pl
from jax.experimental.pallas import tpu as pltpu
from jax.sharding import PartitionSpec as P

MESH = pl.DeviceIdType.MESH
UNROLL_LIMIT = 16
F32 = jnp.float32
BF16 = jnp.bfloat16


def each(start, stop, body):
    if stop - start <= UNROLL_LIMIT:
        for i in range(start, stop):
            body(i)
    else:

        def step(i, carry):
            body(i)
            return carry

        lax.fori_loop(start, stop, step, 0)


def kernel(
    n_mem, n_tile, lib_chunks, block_chunk,
    count_ref, state_hbm, lib_hbm, kind_hbm, column_hbm, value_hbm, error_hbm, frac_hbm,
    gram_ref, proj_ref,
    state_ref, lib_ref, kind_ref, column_ref, value_ref, error_ref, frac_ref,
    prior_ref, regrouped_ref, factor_ref, mean_ref, pert_ref, pert16_ref, weighted_ref,
    piece_ref, landed_ref,
    load_sem, lib_sem, send_sem, recv_sem, piece_send_sem, piece_recv_sem,
):
    mem_dev, value_rows, _ = state_ref.shape
    kind_count, obs_width, _ = lib_ref.shape
    per_block, tile_blocks = kind_ref.shape
    own_blocks = tile_blocks // n_mem
    row_count = own_blocks * obs_width
    members = n_mem * mem_dev
    group = n_mem * n_tile
    mem_id = lax.axis_index("mem")
    tile_id = lax.axis_index("tile")
    me = mem_id * n_tile + tile_id

    def far_first(rank):
        return jnp.where(2 * mem_id < n_mem, n_mem - 1 - rank, rank)

    def to_group(body):
        def row(rank):
            peer_mem = far_first(rank)

            @pl.when(peer_mem != mem_id)
            def _():
                body(peer_mem, tile_id)

            each(1, n_tile, lambda shift: body(peer_mem, lax.rem(tile_id + shift, n_tile)))

        each(0, n_mem, row)

    def to_column(body):
        def one(rank):
            peer_mem = far_first(rank)

            @pl.when(peer_mem != mem_id)
            def _():
                body(peer_mem)

        each(0, n_mem, one)

    barrier = pltpu.get_barrier_semaphore()

    def greet(peer_mem, peer_tile):
        pl.semaphore_signal(
            barrier, inc=1, device_id={"mem": peer_mem, "tile": peer_tile}, device_id_type=MESH
        )

    to_group(greet)

    loads = [
        pltpu.make_async_copy(src, dst, load_sem.at[i])
        for i, (src, dst) in enumerate(
            (
                (kind_hbm, kind_ref), (column_hbm, column_ref), (state_hbm, state_ref),
                (value_hbm, value_ref), (error_hbm, error_ref), (frac_hbm, frac_ref),
            )
        )
    ]
    per_chunk = kind_count // lib_chunks
    lib_loads = [
        pltpu.make_async_copy(
            lib_hbm.at[pl.ds(i * per_chunk, per_chunk)],
            lib_ref.at[pl.ds(i * per_chunk, per_chunk)],
            lib_sem.at[i],
        )
        for i in range(lib_chunks)
    ]
    for copy in loads[:3] + lib_loads + loads[3:]:
        copy.start()

    loads[0].wait()
    loads[1].wait()
    loads[2].wait()

    def priors(first_block, wait_lib):
        kinds = kind_ref[:, pl.ds(first_block, block_chunk)]
        columns = column_ref[:, pl.ds(first_block, block_chunk)]
        entry = lax.broadcasted_iota(jnp.int32, (kind_count, block_chunk), 0)
        chosen = jnp.full((kind_count, block_chunk), -1, jnp.int32)
        for k in range(per_block):
            chosen = jnp.where(kinds[k : k + 1, :] == entry, columns[k : k + 1, :], chosen)
        chosen = jnp.transpose(chosen.astype(F32), (1, 0))
        lane = lax.broadcasted_iota(jnp.int32, (block_chunk, value_rows), 1).astype(F32)
        total = jnp.zeros((mem_dev * block_chunk, obs_width), F32)
        for j in range(kind_count):
            pick = jnp.where(chosen[:, j : j + 1] == lane, 1.0, 0.0).astype(BF16)
            picked = jnp.concatenate(
                [
                    jnp.dot(pick, state_ref[m], preferred_element_type=F32).astype(BF16)
                    for m in range(mem_dev)
                ],
                axis=0,
            )
            if wait_lib and j % per_chunk == 0:
                lib_loads[j // per_chunk].wait()
            total = total + lax.dot_general(
                picked, lib_ref[j], (((1,), (1,)), ((), ())), preferred_element_type=F32
            )
        total = total.astype(BF16).reshape(mem_dev, block_chunk, obs_width)
        prior_ref[:, pl.ds(first_block, block_chunk), :] = total

    if tile_blocks == block_chunk:
        priors(0, True)
    else:
        for copy in lib_loads:
            copy.wait()
        each(0, tile_blocks // block_chunk, lambda i: priors(i * block_chunk, False))

    pl.semaphore_wait(barrier, group - 1)

    def regroup(peer, slot):
        return pltpu.make_async_remote_copy(
            src_ref=prior_ref.at[:, pl.ds(pl.multiple_of(peer * own_blocks, own_blocks), own_blocks), :],
            dst_ref=regrouped_ref.at[slot],
            send_sem=send_sem.at[peer],
            recv_sem=recv_sem.at[slot],
            device_id={"mem": peer},
            device_id_type=MESH,
        )

    to_column(lambda peer: regroup(peer, mem_id).start())
    regrouped_ref[mem_id] = prior_ref[:, pl.ds(pl.multiple_of(mem_id * own_blocks, own_blocks), own_blocks), :]

    for copy in loads[3:]:
        copy.wait()
    target = lax.broadcasted_iota(jnp.int32, (n_tile, row_count), 0).astype(F32) + 0.5
    position = tile_id.astype(F32) + frac_ref[...]
    spread = jnp.abs(position - target)
    distance = jnp.minimum(spread, n_tile - spread) / (n_tile / 4.0)
    error = error_ref[...]
    live = mem_id * row_count + lax.broadcasted_iota(jnp.int32, (1, row_count), 1) < count_ref[0]
    inv_var = jnp.where(live, 1.0 / (error * error), 0.0)
    obs_total = float(n_tile * tile_blocks * obs_width)
    factor_ref[...] = inv_var / (1.0 + distance * distance) / obs_total

    to_column(lambda peer: regroup(peer, peer).wait_recv())

    observed = regrouped_ref[...].astype(F32).reshape(members, own_blocks, obs_width)
    mean = jnp.sum(observed, axis=0) / members
    mean_ref[...] = mean
    pert = (observed - mean[None]).astype(BF16).astype(F32)
    pert_ref[...] = pert.reshape(members * own_blocks, obs_width)

    proj = [jnp.zeros((members, obs_width), F32) for _ in range(n_tile)]
    for b in range(own_blocks):
        lanes = slice(b * obs_width, (b + 1) * obs_width)
        block = pert_ref[pl.ds(b, members, stride=own_blocks), :]
        factor = factor_ref[:, lanes]
        innovation = value_ref[:, lanes] - mean_ref[b : b + 1, :]
        pull = factor * innovation
        pert16_ref[:, lanes] = block.astype(BF16)
        weighted_ref[:, lanes] = jnp.concatenate(
            [block * factor[s : s + 1, :] for s in range(n_tile)], axis=0
        ).astype(BF16)
        for s in range(n_tile):
            proj[s] = proj[s] + block * pull[s : s + 1, :]
    gram = lax.dot_general(
        weighted_ref[...], pert16_ref[...], (((1,), (1,)), ((), ())), preferred_element_type=F32
    )
    for s in range(n_tile):
        sums = jnp.sum(proj[s], axis=1, keepdims=True)
        for i in range(n_mem):
            rows = slice(i * mem_dev, (i + 1) * mem_dev)
            piece_ref[s, i, :, 0:members] = gram[s * members : (s + 1) * members][rows]
            piece_ref[s, i, :, members : members + 1] = sums[rows]

    def share(peer_mem, peer_tile, slot):
        peer = peer_mem * n_tile + peer_tile
        return pltpu.make_async_remote_copy(
            src_ref=piece_ref.at[peer_tile, peer_mem],
            dst_ref=landed_ref.at[slot],
            send_sem=piece_send_sem.at[peer],
            recv_sem=piece_recv_sem.at[slot],
            device_id={"mem": peer_mem, "tile": peer_tile},
            device_id_type=MESH,
        )

    to_group(lambda peer_mem, peer_tile: share(peer_mem, peer_tile, me).start())
    landed_ref[me] = piece_ref[tile_id, mem_id]
    to_column(lambda peer: regroup(peer, mem_id).wait_send())
    to_group(lambda peer_mem, peer_tile: share(peer_mem, peer_tile, peer_mem * n_tile + peer_tile).wait_recv())
    result = jnp.sum(landed_ref[...], axis=0)
    gram_ref[...] = result[:, None, 0:members]
    for m in range(mem_dev):
        proj_ref[0:1, m : m + 1] = result[m : m + 1, members : members + 1]
    to_group(lambda peer_mem, peer_tile: share(peer_mem, peer_tile, me).wait_send())


def on_device(
    state, op_blocks, block_kind, block_column, obs_value, obs_error, obs_frac, obs_count
):
    n_mem = lax.axis_size("mem")
    n_tile = lax.axis_size("tile")
    mem_dev = state.shape[0]
    kind_count, obs_width, _ = op_blocks.shape
    tile_blocks, per_block = block_kind.shape
    own_blocks = tile_blocks // n_mem
    row_count = own_blocks * obs_width
    members = n_mem * mem_dev
    group = n_mem * n_tile
    lib_chunks = 4 if kind_count % 4 == 0 else 1
    block_chunk = 128 if tile_blocks % 128 == 0 else tile_blocks
    piece_width = -(-(members + 1) // 128) * 128
    in_hbm = pl.BlockSpec(memory_space=pltpu.HBM)
    gram, proj = pl.pallas_call(
        functools.partial(kernel, n_mem, n_tile, lib_chunks, block_chunk),
        out_shape=(
            jax.ShapeDtypeStruct((mem_dev, 1, members), F32),
            jax.ShapeDtypeStruct((1, mem_dev), F32),
        ),
        in_specs=[pl.BlockSpec(memory_space=pltpu.SMEM)] + [in_hbm] * 7,
        out_specs=(
            pl.BlockSpec(memory_space=pltpu.VMEM),
            pl.BlockSpec(memory_space=pltpu.VMEM),
        ),
        scratch_shapes=[
            pltpu.VMEM(state.shape, BF16),
            pltpu.VMEM(op_blocks.shape, BF16),
            pltpu.VMEM((per_block, tile_blocks), jnp.int32),
            pltpu.VMEM((per_block, tile_blocks), jnp.int32),
            pltpu.VMEM((1, row_count), F32),
            pltpu.VMEM((1, row_count), F32),
            pltpu.VMEM((1, row_count), F32),
            pltpu.VMEM((mem_dev, tile_blocks, obs_width), BF16),
            pltpu.VMEM((n_mem, mem_dev, own_blocks, obs_width), BF16),
            pltpu.VMEM((n_tile, row_count), F32),
            pltpu.VMEM((own_blocks, obs_width), F32),
            pltpu.VMEM((members * own_blocks, obs_width), F32),
            pltpu.VMEM((members, row_count), BF16),
            pltpu.VMEM((n_tile * members, row_count), BF16),
            pltpu.VMEM((n_tile, n_mem, mem_dev, piece_width), F32),
            pltpu.VMEM((group, mem_dev, piece_width), F32),
            pltpu.SemaphoreType.DMA((6,)),
            pltpu.SemaphoreType.DMA((lib_chunks,)),
            pltpu.SemaphoreType.DMA((n_mem,)),
            pltpu.SemaphoreType.DMA((n_mem,)),
            pltpu.SemaphoreType.DMA((group,)),
            pltpu.SemaphoreType.DMA((group,)),
        ],
        compiler_params=pltpu.CompilerParams(
            collective_id=0, has_side_effects=True, vmem_limit_bytes=40 * 1024 * 1024
        ),
    )(
        obs_count,
        *(
            pltpu.with_memory_space_constraint(array, pltpu.HBM)
            for array in (
                state, op_blocks, jnp.transpose(block_kind), jnp.transpose(block_column),
                obs_value, obs_error, obs_frac,
            )
        ),
    )
    return gram, jnp.transpose(proj)


def solution(mesh):
    return jax.shard_map(
        on_device,
        mesh=mesh,
        in_specs=(
            P(("grp", "mem"), "tile", None),
            P(),
            P(("grp", "tile"), None),
            P(("grp", "tile"), None),
            P(("grp", "tile"), "mem"),
            P(("grp", "tile"), "mem"),
            P(("grp", "tile"), "mem"),
            P(("grp", "tile")),
        ),
        out_specs=(P(("grp", "mem"), "tile", None), P(("grp", "mem"), "tile")),
        check_vma=False,
    )
```

```python
import functools

import jax
import jax.numpy as jnp
from jax import lax
from jax.experimental import pallas as pl
from jax.experimental.pallas import tpu as pltpu
from jax.sharding import PartitionSpec as P

MESH = pl.DeviceIdType.MESH
UNROLL_LIMIT = 16
F32 = jnp.float32
BF16 = jnp.bfloat16


def each(start, stop, body):
    if stop - start <= UNROLL_LIMIT:
        for i in range(start, stop):
            body(i)
    else:

        def step(i, carry):
            body(i)
            return carry

        lax.fori_loop(start, stop, step, 0)


def kernel(
    n_mem, n_tile, n_host, lib_chunks, block_chunk,
    count_ref, state_hbm, lib_hbm, kind_hbm, column_hbm, value_hbm, error_hbm, frac_hbm,
    gram_ref, proj_ref,
    state_ref, lib_ref, kind_ref, column_ref, own_obs_ref, obs_ref,
    prior_ref, regrouped_ref, factor_ref, mean_ref, pert_ref, pert16_ref, weighted_ref,
    piece_ref, landed_ref,
    load_sem, lib_sem, send_sem, recv_sem, obs_send_sem, obs_recv_sem, piece_send_sem, piece_recv_sem,
):
    mem_dev, value_rows, _ = state_ref.shape
    kind_count, obs_width, _ = lib_ref.shape
    per_block, tile_blocks = kind_ref.shape
    own_blocks = tile_blocks // n_mem
    row_count = own_blocks * obs_width
    members = n_mem * mem_dev
    group = n_mem * n_tile
    mem_id = lax.axis_index("mem")
    tile_id = lax.axis_index("tile")
    me = mem_id * n_tile + tile_id
    per_host = n_mem // n_host
    first_host = (n_mem - n_host) // 2
    host = mem_id - first_host
    is_host = jnp.logical_and(mem_id >= first_host, mem_id < first_host + n_host)
    my_host = first_host + mem_id // per_host
    host_blocks = own_blocks * per_host

    def far_first(rank, first, count):
        return jnp.where(2 * mem_id < n_mem, first + count - 1 - rank, first + rank)

    def to_row(peer_mem, body):
        @pl.when(peer_mem != mem_id)
        def _():
            body(peer_mem, tile_id)

        each(1, n_tile, lambda shift: body(peer_mem, lax.rem(tile_id + shift, n_tile)))

    def to_group(body):
        each(0, n_mem, lambda rank: to_row(far_first(rank, 0, n_mem), body))

    def to_hosts(body):
        each(0, n_host, lambda rank: to_row(far_first(rank, first_host, n_host), body))

    def to_column(first, count, body):
        def one(rank):
            peer_mem = far_first(rank, first, count)

            @pl.when(peer_mem != mem_id)
            def _():
                body(peer_mem)

        each(0, count, one)

    barrier = pltpu.get_barrier_semaphore()

    def greet(peer_mem, peer_tile):
        pl.semaphore_signal(
            barrier, inc=1, device_id={"mem": peer_mem, "tile": peer_tile}, device_id_type=MESH
        )

    def greet_column(peer_mem):
        @pl.when(jnp.logical_or(peer_mem < first_host, peer_mem >= first_host + n_host))
        def _():
            greet(peer_mem, tile_id)

    @pl.when(is_host)
    def _():
        to_column(0, n_mem, greet_column)

    to_hosts(greet)

    loads = [
        pltpu.make_async_copy(src, dst, load_sem.at[i])
        for i, (src, dst) in enumerate(
            (
                (kind_hbm, kind_ref), (column_hbm, column_ref), (state_hbm, state_ref),
                (value_hbm, own_obs_ref.at[0]), (error_hbm, own_obs_ref.at[1]), (frac_hbm, own_obs_ref.at[2]),
            )
        )
    ]
    per_chunk = kind_count // lib_chunks
    lib_loads = [
        pltpu.make_async_copy(
            lib_hbm.at[pl.ds(i * per_chunk, per_chunk)],
            lib_ref.at[pl.ds(i * per_chunk, per_chunk)],
            lib_sem.at[i],
        )
        for i in range(lib_chunks)
    ]
    for copy in loads + lib_loads:
        copy.start()

    for copy in loads:
        copy.wait()

    def obs_to_host(owner):
        return pltpu.make_async_remote_copy(
            src_ref=own_obs_ref,
            dst_ref=obs_ref.at[lax.rem(owner, per_host)],
            send_sem=obs_send_sem.at[0],
            recv_sem=obs_recv_sem.at[lax.rem(owner, per_host)],
            device_id={"mem": my_host},
            device_id_type=MESH,
        )

    @pl.when(jnp.logical_not(is_host))
    def _():
        pl.semaphore_wait(barrier, n_host)

    @pl.when(jnp.logical_and(jnp.logical_not(is_host), my_host != mem_id))
    def _():
        obs_to_host(mem_id).start()

    def priors(first_block, wait_lib):
        kinds = kind_ref[:, pl.ds(first_block, block_chunk)]
        columns = column_ref[:, pl.ds(first_block, block_chunk)]
        entry = lax.broadcasted_iota(jnp.int32, (kind_count, block_chunk), 0)
        chosen = jnp.full((kind_count, block_chunk), -1, jnp.int32)
        for k in range(per_block):
            chosen = jnp.where(kinds[k : k + 1, :] == entry, columns[k : k + 1, :], chosen)
        chosen = jnp.transpose(chosen.astype(F32), (1, 0))
        lane = lax.broadcasted_iota(jnp.int32, (block_chunk, value_rows), 1).astype(F32)
        total = jnp.zeros((mem_dev * block_chunk, obs_width), F32)
        for j in range(kind_count):
            pick = jnp.where(chosen[:, j : j + 1] == lane, 1.0, 0.0).astype(BF16)
            picked = jnp.concatenate(
                [
                    jnp.dot(pick, state_ref[m], preferred_element_type=F32).astype(BF16)
                    for m in range(mem_dev)
                ],
                axis=0,
            )
            if wait_lib and j % per_chunk == 0:
                lib_loads[j // per_chunk].wait()
            total = total + lax.dot_general(
                picked, lib_ref[j], (((1,), (1,)), ((), ())), preferred_element_type=F32
            )
        total = total.astype(BF16).reshape(mem_dev, block_chunk, obs_width)
        prior_ref[:, pl.ds(first_block, block_chunk), :] = total

    if tile_blocks == block_chunk:
        priors(0, True)
    else:
        for copy in lib_loads:
            copy.wait()
        each(0, tile_blocks // block_chunk, lambda i: priors(i * block_chunk, False))

    @pl.when(is_host)
    def _():
        pl.semaphore_wait(barrier, group - 1)

    @pl.when(jnp.logical_and(is_host, my_host != mem_id))
    def _():
        obs_to_host(mem_id).start()

    def host_rows_of(peer_mem):
        return pl.ds(pl.multiple_of((peer_mem - first_host) * host_blocks, host_blocks), host_blocks)

    def regroup(peer, slot):
        return pltpu.make_async_remote_copy(
            src_ref=prior_ref.at[:, host_rows_of(peer), :],
            dst_ref=regrouped_ref.at[slot],
            send_sem=send_sem.at[peer],
            recv_sem=recv_sem.at[slot],
            device_id={"mem": peer},
            device_id_type=MESH,
        )

    def regroup_arriving(slot):
        return pltpu.make_async_remote_copy(
            src_ref=prior_ref.at[:, pl.ds(0, host_blocks), :],
            dst_ref=regrouped_ref.at[slot],
            send_sem=send_sem.at[slot],
            recv_sem=recv_sem.at[slot],
            device_id={"mem": slot},
            device_id_type=MESH,
        )

    to_column(first_host, n_host, lambda peer: regroup(peer, mem_id).start())

    def share(peer_mem, peer_tile, slot):
        return pltpu.make_async_remote_copy(
            src_ref=piece_ref.at[peer_tile, peer_mem],
            dst_ref=landed_ref.at[slot],
            send_sem=piece_send_sem.at[peer_mem * n_tile + peer_tile],
            recv_sem=piece_recv_sem.at[slot],
            device_id={"mem": peer_mem, "tile": peer_tile},
            device_id_type=MESH,
        )

    @pl.when(is_host)
    def _():
        regrouped_ref[mem_id] = prior_ref[:, host_rows_of(mem_id), :]

        target = lax.broadcasted_iota(jnp.int32, (n_tile, row_count), 0).astype(F32) + 0.5
        obs_total = float(n_tile * tile_blocks * obs_width)
        for part in range(per_host):
            owner = host * per_host + part

            @pl.when(owner == mem_id)
            def _():
                obs_ref[part] = own_obs_ref[...]

            @pl.when(owner != mem_id)
            def _():
                obs_to_host(owner).wait_recv()

            spread = jnp.abs(tile_id.astype(F32) + obs_ref[part, 2] - target)
            distance = jnp.minimum(spread, n_tile - spread) / (n_tile / 4.0)
            error = obs_ref[part, 1]
            row = lax.broadcasted_iota(jnp.int32, (1, row_count), 1)
            live = owner * row_count + row < count_ref[0]
            inv_var = jnp.where(live, 1.0 / (error * error), 0.0)
            factor_ref[:, part * row_count : (part + 1) * row_count] = (
                inv_var / (1.0 + distance * distance) / obs_total
            )

        to_column(0, n_mem, lambda peer: regroup_arriving(peer).wait_recv())

        observed = regrouped_ref[...].astype(F32).reshape(members, host_blocks, obs_width)
        mean = jnp.sum(observed, axis=0) / members
        mean_ref[...] = mean
        pert = (observed - mean[None]).astype(BF16).astype(F32)
        pert_ref[...] = pert.reshape(members * host_blocks, obs_width)

        proj = [jnp.zeros((members, obs_width), F32) for _ in range(n_tile)]
        for b in range(host_blocks):
            lanes = slice(b * obs_width, (b + 1) * obs_width)
            part, part_block = divmod(b, own_blocks)
            part_lanes = slice(part_block * obs_width, (part_block + 1) * obs_width)
            block = pert_ref[pl.ds(b, members, stride=host_blocks), :]
            factor = factor_ref[:, lanes]
            innovation = obs_ref[part, 0, :, part_lanes] - mean_ref[b : b + 1, :]
            pull = factor * innovation
            pert16_ref[:, lanes] = block.astype(BF16)
            weighted_ref[:, lanes] = jnp.concatenate(
                [block * factor[s : s + 1, :] for s in range(n_tile)], axis=0
            ).astype(BF16)
            for s in range(n_tile):
                proj[s] = proj[s] + block * pull[s : s + 1, :]
        gram = lax.dot_general(
            weighted_ref[...], pert16_ref[...], (((1,), (1,)), ((), ())), preferred_element_type=F32
        )
        for s in range(n_tile):
            sums = jnp.sum(proj[s], axis=1, keepdims=True)
            for i in range(n_mem):
                rows = slice(i * mem_dev, (i + 1) * mem_dev)
                piece_ref[s, i, :, 0:members] = gram[s * members : (s + 1) * members][rows]
                piece_ref[s, i, :, members : members + 1] = sums[rows]

        slot = host * n_tile + tile_id
        to_group(lambda peer_mem, peer_tile: share(peer_mem, peer_tile, slot).start())
        landed_ref[slot] = piece_ref[tile_id, mem_id]

    to_column(first_host, n_host, lambda peer: regroup(peer, mem_id).wait_send())

    @pl.when(my_host != mem_id)
    def _():
        obs_to_host(mem_id).wait_send()

    to_hosts(
        lambda peer_mem, peer_tile: share(
            peer_mem, peer_tile, (peer_mem - first_host) * n_tile + peer_tile
        ).wait_recv()
    )
    result = jnp.sum(landed_ref[...], axis=0)
    gram_ref[...] = result[:, None, 0:members]
    for m in range(mem_dev):
        proj_ref[0:1, m : m + 1] = result[m : m + 1, members : members + 1]

    @pl.when(is_host)
    def _():
        to_group(lambda peer_mem, peer_tile: share(peer_mem, peer_tile, 0).wait_send())


def on_device(
    state, op_blocks, block_kind, block_column, obs_value, obs_error, obs_frac, obs_count
):
    n_mem = lax.axis_size("mem")
    n_tile = lax.axis_size("tile")
    mem_dev = state.shape[0]
    kind_count, obs_width, _ = op_blocks.shape
    tile_blocks, per_block = block_kind.shape
    own_blocks = tile_blocks // n_mem
    row_count = own_blocks * obs_width
    members = n_mem * mem_dev
    group = n_mem * n_tile
    n_host = n_mem // 2 if n_mem == 4 else n_mem
    per_host = n_mem // n_host
    lib_chunks = 4 if kind_count % 4 == 0 else 1
    block_chunk = 128 if tile_blocks % 128 == 0 else tile_blocks
    piece_width = -(-(members + 1) // 128) * 128
    in_hbm = pl.BlockSpec(memory_space=pltpu.HBM)
    gram, proj = pl.pallas_call(
        functools.partial(kernel, n_mem, n_tile, n_host, lib_chunks, block_chunk),
        out_shape=(
            jax.ShapeDtypeStruct((mem_dev, 1, members), F32),
            jax.ShapeDtypeStruct((1, mem_dev), F32),
        ),
        in_specs=[pl.BlockSpec(memory_space=pltpu.SMEM)] + [in_hbm] * 7,
        out_specs=(
            pl.BlockSpec(memory_space=pltpu.VMEM),
            pl.BlockSpec(memory_space=pltpu.VMEM),
        ),
        scratch_shapes=[
            pltpu.VMEM(state.shape, BF16),
            pltpu.VMEM(op_blocks.shape, BF16),
            pltpu.VMEM((per_block, tile_blocks), jnp.int32),
            pltpu.VMEM((per_block, tile_blocks), jnp.int32),
            pltpu.VMEM((3, 1, row_count), F32),
            pltpu.VMEM((per_host, 3, 1, row_count), F32),
            pltpu.VMEM((mem_dev, tile_blocks, obs_width), BF16),
            pltpu.VMEM((n_mem, mem_dev, own_blocks * per_host, obs_width), BF16),
            pltpu.VMEM((n_tile, row_count * per_host), F32),
            pltpu.VMEM((own_blocks * per_host, obs_width), F32),
            pltpu.VMEM((members * own_blocks * per_host, obs_width), F32),
            pltpu.VMEM((members, row_count * per_host), BF16),
            pltpu.VMEM((n_tile * members, row_count * per_host), BF16),
            pltpu.VMEM((n_tile, n_mem, mem_dev, piece_width), F32),
            pltpu.VMEM((n_host * n_tile, mem_dev, piece_width), F32),
            pltpu.SemaphoreType.DMA((6,)),
            pltpu.SemaphoreType.DMA((lib_chunks,)),
            pltpu.SemaphoreType.DMA((n_mem,)),
            pltpu.SemaphoreType.DMA((n_mem,)),
            pltpu.SemaphoreType.DMA((1,)),
            pltpu.SemaphoreType.DMA((per_host,)),
            pltpu.SemaphoreType.DMA((group,)),
            pltpu.SemaphoreType.DMA((n_host * n_tile,)),
        ],
        compiler_params=pltpu.CompilerParams(
            collective_id=0, has_side_effects=True, vmem_limit_bytes=40 * 1024 * 1024
        ),
    )(
        obs_count,
        *(
            pltpu.with_memory_space_constraint(array, pltpu.HBM)
            for array in (
                state, op_blocks, jnp.transpose(block_kind), jnp.transpose(block_column),
                obs_value, obs_error, obs_frac,
            )
        ),
    )
    return gram, jnp.transpose(proj)


def solution(mesh):
    return jax.shard_map(
        on_device,
        mesh=mesh,
        in_specs=(
            P(("grp", "mem"), "tile", None),
            P(),
            P(("grp", "tile"), None),
            P(("grp", "tile"), None),
            P(("grp", "tile"), "mem"),
            P(("grp", "tile"), "mem"),
            P(("grp", "tile"), "mem"),
            P(("grp", "tile")),
        ),
        out_specs=(P(("grp", "mem"), "tile", None), P(("grp", "mem"), "tile")),
        check_vma=False,
    )
```
